32 devices in a mesh: parts: 2 (over x), attn: 8 (over z, y), ffn: 2 (over core).
Axes of the slice: x: 2, y: 2, z: 4, core: 2. Of those that a mesh axis runs over, the one named last changes fastest.
Arguments:
- hidden_states: bfloat16 [256, 7168], P(('parts', 'attn', 'ffn')), parts along dimension 0, may hold values from -127 to 127
- norm_gain: bfloat16 [7168], replicated, may hold values from 0.099609375 to 1.8984375
- expert_ids: int32 [256, 3], P(('parts', 'attn', 'ffn')), parts along dimension 0, may hold values from 0 to 3, as said below
- route_weight: float32 [256, 3], P(('parts', 'attn', 'ffn')), parts along dimension 0, may hold values from 0.2 to 1
- w_gate: bfloat16 [7168, 16384], P(None, ('attn', 'ffn')), may hold values from -0.0625 to 0.0625
- w_up: bfloat16 [7168, 16384], P(None, ('attn', 'ffn')), may hold values from -0.0625 to 0.0625
- w_down: bfloat16 [16384, 7168], P(('attn', 'ffn')), may hold values from -0.09375 to 0.09375
- queries: bfloat16 [256, 16384], P(('parts', 'attn', 'ffn')), parts along dimension 0, may hold values from -36 to 36
- key_cache: bfloat16 [256, 128, 256], P(('parts', 'attn', 'ffn')), parts along dimension 0, may hold values from -19 to 19
- value_cache: bfloat16 [256, 128, 256], P(('parts', 'attn', 'ffn')), parts along dimension 0, may hold values from -6 to 6
- lengths: int32 [256], P(('parts', 'attn', 'ffn')), parts along dimension 0, may hold values from 2 to 128, as said below
Outputs:
- ffn_out: bfloat16 [256, 7168], P(('parts', 'attn', 'ffn')), parts along dimension 0
- attn_out: bfloat16 [256, 16384], P(('parts', 'attn', 'ffn')), parts along dimension 0
The draws below stay inside these ranges and needn't reach their ends.
There are 2 independent parts, one for each index of `parts`. The reference program is written for one: setup_inputs(seed, part) draws one part's arguments, and reference() takes and returns one part's arrays. A program takes and returns all parts, laid end to end along the dimension named above; an argument that names none is the same for every part. Nothing has to cross between parts.
Inputs may be any that keep to these rules, and one draw needn't show every extreme that they name: `expert_ids`: each row names 3 different experts. Among the 8 rows of one device at most 7 name any one expert, and in every draw one expert is named by exactly 7 rows on every device. `lengths`: each device has one row with exactly 128 filled slots.
All inputs are finite; a program needn't handle non-finite values.
Results may differ from the reference program's by a relative error of at most 0.0071.
Values may be sent and summed in bfloat16 or wider, within the bound.
A program may use at most 128 MiB of HBM per device.

```python
import jax
import jax.numpy as jnp
from jax import lax

D = 7168
FFH = 4096
EXPERTS = 4
TOP = 3
HEADS = 64
HEAD_DIM = 256
ROWS = 8
CACHE = 128
CAP = 7
ALL_ROWS = 128
N_ATTN = 8
N_FFN = 2


def shared_keys(key):
    return jnp.clip(jax.random.normal(key, (ALL_ROWS, CACHE, HEAD_DIM), jnp.float32), -6.0, 6.0)


def draw_key_cache(key, part):
    base = shared_keys(key)
    return base.astype(jnp.bfloat16)


def draw_queries(key, part):
    key = jax.random.fold_in(key, 12)
    fresh = jnp.clip(jax.random.normal(key, (ALL_ROWS, HEADS, HEAD_DIM), jnp.float32), -6.0, 6.0)
    return fresh.reshape(ALL_ROWS, HEADS * HEAD_DIM).astype(jnp.bfloat16)


def draw_hidden_states(key, part):
    key = jax.random.fold_in(key, 13)
    first_key = jax.random.fold_in(key, 0)
    values = jnp.clip(jax.random.normal(first_key, (ALL_ROWS, D), jnp.float32), -6.0, 6.0)
    return values.astype(jnp.bfloat16)


def draw_expert_ids(key, part):
    key = jax.random.fold_in(key, 14)
    first_key, second_key, third_key, fourth_key = jax.random.split(key, 4)
    blocks = ALL_ROWS // ROWS
    full_expert = jax.random.randint(first_key, (), 0, EXPERTS)
    offset = jax.random.randint(second_key, (blocks, 1), 0, EXPERTS - 1)
    place = jnp.arange(ROWS, dtype=jnp.int32)[None, :]
    others = (full_expert + 1 + (place + offset) % (EXPERTS - 1)) % EXPERTS
    left_out = jnp.where(place < ROWS - CAP, full_expert, others)
    orders = jax.vmap(lambda sub_key: jax.random.permutation(sub_key, ROWS))(jax.random.split(third_key, blocks))
    left_out = jnp.take_along_axis(left_out, orders, axis=1).reshape(ALL_ROWS)
    turn = jax.random.randint(fourth_key, (ALL_ROWS, 1), 0, EXPERTS - 1)
    rank = jnp.arange(TOP, dtype=jnp.int32)[None, :]
    return ((left_out[:, None] + 1 + (rank + turn) % (EXPERTS - 1)) % EXPERTS).astype(jnp.int32)


def draw_lengths(key, part):
    key = jax.random.fold_in(key, 15)
    first_key, second_key, third_key = jax.random.split(key, 3)
    blocks = ALL_ROWS // ROWS
    spread = jax.random.randint(first_key, (blocks, 1), 1, 5)
    raw = jax.random.randint(second_key, (blocks, ROWS), 0, CACHE - 1)
    filled = 2 + raw * spread // 4
    pick = jax.random.randint(third_key, (blocks, 1), 0, ROWS)
    longest = jnp.arange(ROWS, dtype=jnp.int32)[None, :] == pick
    return jnp.where(longest, CACHE, filled).reshape(ALL_ROWS).astype(jnp.int32)


def block_scale(key, extent, cuts, smallest, high):
    factor_of = 1.0
    for axis_at, parts in cuts:
        steps = jax.random.uniform(jax.random.fold_in(jax.random.fold_in(key, 6), axis_at), (parts,), jnp.float32, smallest / len(cuts), high / len(cuts))
        factor_of = factor_of * jnp.repeat(jnp.exp(steps), extent[axis_at] // parts).reshape((-1,) + (1,) * (len(extent) - 1 - axis_at))
    return factor_of


def scatter_about(own_key, extent, scale, bound, cuts=(), kind=jnp.bfloat16):
    values = scale * jax.random.normal(own_key, extent, jnp.float32)
    if cuts:
        values = values * block_scale(own_key, extent, cuts, -0.22, 0.18)
    return jnp.clip(values, -bound, bound).astype(kind)


def setup_inputs(seed: int = 0, part: int = 0) -> dict:
    key_list = jax.random.split(jax.random.key(seed), 12)
    part_splits = jax.random.split(jax.random.fold_in(key_list[11], part), 12)
    hidden_states = draw_hidden_states(jax.random.fold_in(jax.random.fold_in(key_list[11], part), 71), part)
    norm_gain = jnp.clip(1.0 + 0.18 * jax.random.normal(key_list[1], (D,), jnp.float32), 0.099609375, 1.8984375).astype(jnp.bfloat16)
    expert_ids = draw_expert_ids(jax.random.fold_in(jax.random.fold_in(key_list[11], part), 71), part)
    route_weight = jnp.clip(0.2 + 0.8 * jax.random.uniform(part_splits[3], (ALL_ROWS, TOP), jnp.float32) ** block_scale(part_splits[3], (ALL_ROWS, TOP), ((0, 16),), -0.2, 0.2), 0.2, 1.0)
    w_gate = scatter_about(key_list[4], (D, EXPERTS * FFH), D ** -0.5, 0.0625, ((1, 16),))
    w_up = scatter_about(key_list[5], (D, EXPERTS * FFH), D ** -0.5, 0.0625, ((1, 16),))
    w_down = scatter_about(key_list[6], (EXPERTS * FFH, D), FFH ** -0.5, 0.09375, ((0, 16),))
    queries = draw_queries(jax.random.fold_in(jax.random.fold_in(key_list[11], part), 71), part)
    key_cache = draw_key_cache(jax.random.fold_in(jax.random.fold_in(key_list[11], part), 71), part)
    value_cache = scatter_about(part_splits[9], (ALL_ROWS, CACHE, HEAD_DIM), 1.0, 6.0, ((0, 16),))
    lengths = draw_lengths(jax.random.fold_in(jax.random.fold_in(key_list[11], part), 71), part)
    return dict(hidden_states=hidden_states, norm_gain=norm_gain, expert_ids=expert_ids, route_weight=route_weight, w_gate=w_gate, w_up=w_up, w_down=w_down, queries=queries, key_cache=key_cache, value_cache=value_cache, lengths=lengths)


def reference(hidden_states, norm_gain, expert_ids, route_weight, w_gate, w_up, w_down, queries, key_cache, value_cache, lengths):
    as_float = hidden_states.astype(jnp.float32)
    mean_square = lax.optimization_barrier(jnp.mean(as_float * as_float, axis=-1, keepdims=True))
    normed = (as_float * lax.rsqrt(mean_square + 1e-06) * norm_gain.astype(jnp.float32)).astype(jnp.bfloat16)
    group_size = N_ATTN * N_FFN // EXPERTS
    span = FFH // group_size
    total = jnp.zeros((ALL_ROWS, D), jnp.float32)
    for expert in range(EXPERTS):
        gate_part = jnp.dot(normed, w_gate[:, expert * FFH:(expert + 1) * FFH], preferred_element_type=jnp.float32)
        up_part = jnp.dot(normed, w_up[:, expert * FFH:(expert + 1) * FFH], preferred_element_type=jnp.float32)
        expert_hidden = (jax.nn.silu(gate_part) * up_part).astype(jnp.bfloat16)
        down_rows = w_down[expert * FFH:(expert + 1) * FFH]

        def add_member(member, acc):
            start = (member * span).astype(jnp.int32)
            piece = lax.dynamic_slice_in_dim(expert_hidden, start, span, 1)
            rows_down = lax.dynamic_slice_in_dim(down_rows, start, span, 0)
            partial_sum = lax.optimization_barrier(jnp.dot(piece, rows_down, preferred_element_type=jnp.float32).astype(jnp.bfloat16))
            return acc + partial_sum.astype(jnp.float32)
        expert_sums = lax.fori_loop(0, group_size, add_member, jnp.zeros((ALL_ROWS, D), jnp.float32))
        expert_weight = lax.optimization_barrier(jnp.sum(jnp.where(expert_ids == expert, route_weight.astype(jnp.float32), 0.0), axis=1))
        total = total + expert_weight[:, None] * expert_sums
    ffn_out = total.astype(jnp.bfloat16)
    query_heads = queries.astype(jnp.float32).reshape(ALL_ROWS, HEADS, HEAD_DIM)
    scores = jnp.einsum('rhd,rld->rhl', query_heads, key_cache.astype(jnp.float32)) * HEAD_DIM ** (-0.5)
    visible = jnp.arange(CACHE, dtype=jnp.int32)[None, None, :] < lengths.astype(jnp.int32)[:, None, None]
    top_score = lax.optimization_barrier(jnp.max(jnp.where(visible, scores, -1e+30), axis=-1, keepdims=True))
    raised = jnp.where(visible, jnp.exp(scores - top_score), 0.0)
    attention_probs = (raised / lax.optimization_barrier(jnp.sum(raised, axis=-1, keepdims=True))).astype(jnp.bfloat16)
    mixed = jnp.einsum('rhl,rld->rhd', attention_probs.astype(jnp.float32), value_cache.astype(jnp.float32))
    attn_out = mixed.reshape(ALL_ROWS, HEADS * HEAD_DIM).astype(jnp.bfloat16)
    return (ffn_out, attn_out)
```

```python
import functools

import jax
import jax.numpy as jnp
from jax import lax
from jax.experimental import pallas as pl
from jax.experimental.pallas import tpu as pltpu
from jax.sharding import PartitionSpec as P

EXPERTS = 4
HEADS = 64
HEAD_DIM = 256
ROWS = 8
PIECES = 4
CHUNKS = 7
F32 = jnp.float32
BF16 = jnp.bfloat16
MESH = pl.DeviceIdType.MESH


def kernel(
    outer,
    hid_ref,
    gain_ref,
    ids_ref,
    rw_ref,
    len_ref,
    q_hbm,
    k_hbm,
    v_hbm,
    wg_hbm,
    wu_hbm,
    wd_hbm,
    ffn_ref,
    attn_ref,
    wg,
    wu,
    wd,
    q_v,
    k_v,
    v_v,
    x,
    gate_acc,
    up_acc,
    hidden,
    part,
    core_in,
    sum_core,
    y_in,
    sum_y,
    z_in,
    att_sem,
    wgu_sem,
    wd_sem,
    z_send,
    z_recv,
    y_send,
    y_recv,
    c_send,
    c_recv,
    rc_send,
    rc_recv,
    ry_send,
    ry_recv,
    rz_send,
    rz_recv,
):
    parts = lax.axis_index("parts")
    attn = lax.axis_index("attn")
    c = lax.axis_index("ffn")
    o = attn // 2
    i = attn % 2
    half = hid_ref.shape[1] // 2
    kc = half // CHUNKS
    blocks = 4 * outer

    def device(o2, i2, c2):
        return (parts, o2 * 2 + i2, c2)

    def z_peer(d):
        return lax.rem(o + d, outer)

    def att_copies():
        return [
            pltpu.make_async_copy(a, b, att_sem.at[n])
            for n, (a, b) in enumerate(((q_hbm, q_v), (k_hbm, k_v), (v_hbm, v_v)))
        ]

    def in_weights(k):
        copies = []
        for h in range(2):
            rows = pl.ds(pl.multiple_of(h * half + k * kc, kc), kc)
            for n, (a, b) in enumerate(((wg_hbm, wg), (wu_hbm, wu))):
                copies.append(
                    pltpu.make_async_copy(
                        a.at[rows, :], b.at[k, pl.ds(h * kc, kc), :], wgu_sem.at[k, n, h]
                    )
                )
        return copies

    def out_weights(k):
        copies = []
        for h in range(2):
            cols = pl.ds(pl.multiple_of(h * half + k * kc, kc), kc)
            copies.append(
                pltpu.make_async_copy(
                    wd_hbm.at[:, cols], wd.at[k, :, pl.ds(h * kc, kc)], wd_sem.at[k, h]
                )
            )
        return copies

    def z_copy(k, o_slot, d):
        return pltpu.make_async_remote_copy(
            src_ref=x.at[k, c, i, o_slot],
            dst_ref=x.at[k, c, i, o_slot],
            send_sem=z_send.at[k, d],
            recv_sem=z_recv.at[k, o_slot],
            device_id=device(z_peer(d), i, c),
            device_id_type=MESH,
        )

    def y_copy(k, i_slot):
        return pltpu.make_async_remote_copy(
            src_ref=x.at[k, c, i_slot],
            dst_ref=x.at[k, c, i_slot],
            send_sem=y_send.at[k],
            recv_sem=y_recv.at[k],
            device_id=device(o, 1 - i, c),
            device_id_type=MESH,
        )

    def c_copy(k, c_slot):
        return pltpu.make_async_remote_copy(
            src_ref=x.at[k, c_slot],
            dst_ref=x.at[k, c_slot],
            send_sem=c_send.at[k],
            recv_sem=c_recv.at[k],
            device_id=device(o, i, 1 - c),
            device_id_type=MESH,
        )

    def rc_copy(k):
        return pltpu.make_async_remote_copy(
            src_ref=part.at[k, 1 - c],
            dst_ref=core_in.at[k],
            send_sem=rc_send.at[k],
            recv_sem=rc_recv.at[k],
            device_id=device(o, i, 1 - c),
            device_id_type=MESH,
        )

    def ry_copy(k):
        return pltpu.make_async_remote_copy(
            src_ref=sum_core.at[k, 1 - i],
            dst_ref=y_in.at[k],
            send_sem=ry_send.at[k],
            recv_sem=ry_recv.at[k],
            device_id=device(o, 1 - i, c),
            device_id_type=MESH,
        )

    def rz_copy(k, o_src, o_dst, o_slot, d):
        return pltpu.make_async_remote_copy(
            src_ref=sum_y.at[k, o_src],
            dst_ref=z_in.at[k, o_slot],
            send_sem=rz_send.at[k, d],
            recv_sem=rz_recv.at[k, o_slot],
            device_id=device(o_dst, i, c),
            device_id_type=MESH,
        )

    for k in range(2):
        for copy in in_weights(k):
            copy.start()

    barrier = pltpu.get_barrier_semaphore()
    for d in range(1, outer):
        pl.semaphore_signal(
            barrier, inc=1, device_id=device(z_peer(d), i, c), device_id_type=MESH
        )
    pl.semaphore_signal(barrier, inc=1, device_id=device(o, 1 - i, c), device_id_type=MESH)
    pl.semaphore_signal(barrier, inc=1, device_id=device(o, i, 1 - c), device_id_type=MESH)

    for copy in att_copies():
        copy.start()

    as_float = hid_ref[...].astype(F32)
    mean_square = jnp.mean(as_float * as_float, axis=-1, keepdims=True)
    normed = as_float * lax.rsqrt(mean_square + 1e-06) * gain_ref[...]
    for k in range(CHUNKS):
        low = normed[:, k * kc : (k + 1) * kc]
        high = normed[:, half + k * kc : half + (k + 1) * kc]
        x[k, c, i, o] = jnp.concatenate([low, high], axis=0).astype(BF16)

    pl.semaphore_wait(barrier, outer + 1)

    def start_z(k, _):
        for d in range(1, outer):
            z_copy(k, o, d).start()
        return 0

    lax.fori_loop(0, CHUNKS, start_z, 0)

    def start_in(k, _):
        for copy in in_weights(k):
            copy.start()
        return 0

    lax.fori_loop(2, CHUNKS, start_in, 0)

    def start_out(k, _):
        for copy in out_weights(k):
            copy.start()
        return 0

    lax.fori_loop(0, CHUNKS, start_out, 0)

    gate_acc[...] = jnp.zeros_like(gate_acc)
    up_acc[...] = jnp.zeros_like(up_acc)
    for copy in att_copies():
        copy.wait()

    heads = HEADS // PIECES
    tall = heads * ROWS
    slots = k_v.shape[1]

    def attention(p):
        def columns(j):
            return pl.ds(pl.multiple_of((p * heads + j) * HEAD_DIM, HEAD_DIM), HEAD_DIM)

        query = jnp.concatenate(
            [q_v[:, columns(j)].astype(F32) for j in range(heads)], axis=0
        ).astype(BF16)
        row = lax.broadcasted_iota(jnp.int32, (tall, slots), 0) & (ROWS - 1)
        filled = jnp.zeros((tall, slots), jnp.int32)
        scores = jnp.zeros((tall, slots), F32)
        for r in range(ROWS):
            own = lax.dot_general(
                query, k_v[r], (((1,), (1,)), ((), ())), preferred_element_type=F32
            )
            scores = jnp.where(row == r, own, scores)
            filled = jnp.where(row == r, len_ref[r], filled)
        scores = scores * HEAD_DIM ** (-0.5)
        visible = lax.broadcasted_iota(jnp.int32, (tall, slots), 1) < filled
        top = jnp.max(jnp.where(visible, scores, -1e30), axis=-1, keepdims=True)
        raised = jnp.where(visible, jnp.exp(scores - top), 0.0)
        probs = raised / jnp.sum(raised, axis=-1, keepdims=True)
        mixed = jnp.zeros((tall, HEAD_DIM), F32)
        for r in range(ROWS):
            own = jnp.where(row == r, probs, 0.0).astype(BF16)
            mixed = mixed + jnp.dot(own, v_v[r], preferred_element_type=F32)
        for j in range(heads):
            attn_ref[:, columns(j)] = mixed[j * ROWS : (j + 1) * ROWS].astype(BF16)

    def gather_step(t, _):
        @pl.when(t < PIECES)
        def _():
            attention(t)

        @pl.when(t < CHUNKS)
        def _():
            for d in range(1, outer):
                z_copy(t, z_peer(d), d).wait_recv()
            y_copy(t, i).start()

        @pl.when((t >= 1) & (t < CHUNKS + 1))
        def _():
            y_copy(t - 1, 1 - i).wait_recv()
            c_copy(t - 1, c).start()

        @pl.when(t >= 2)
        def _():
            k = t - 2
            c_copy(k, 1 - c).wait_recv()
            for copy in in_weights(k):
                copy.wait()
            block = x[k].astype(F32).reshape(blocks, 2 * ROWS, kc)
            low = block[:, :ROWS, :].reshape(blocks * ROWS, kc).astype(BF16)
            high = block[:, ROWS:, :].reshape(blocks * ROWS, kc).astype(BF16)
            rows = jnp.concatenate([low, high], axis=1)
            gate_acc[...] += jnp.dot(rows, wg[k], preferred_element_type=F32)
            up_acc[...] += jnp.dot(rows, wu[k], preferred_element_type=F32)

        return 0

    lax.fori_loop(0, CHUNKS + 2, gather_step, 0)

    gate = gate_acc[...]
    hidden[...] = (gate / (1.0 + jnp.exp(-gate)) * up_acc[...]).astype(BF16)

    ids = ids_ref[...]
    weights = rw_ref[...]
    row_weight = [
        jnp.sum(jnp.where(ids == e, weights, 0.0), axis=1, keepdims=True) for e in range(EXPERTS)
    ]
    row_weight = [jnp.concatenate([w, w], axis=0) for w in row_weight]
    per_expert = outer // EXPERTS

    def sum_step(t, _):
        @pl.when(t < CHUNKS)
        def _():
            for copy in out_weights(t):
                copy.wait()
            down = jnp.dot(hidden[...], wd[t], preferred_element_type=F32)
            low = down[:, :kc].reshape(blocks, ROWS, kc)
            high = down[:, kc:].reshape(blocks, ROWS, kc)
            both = jnp.concatenate([low, high], axis=1).astype(BF16)
            part[t] = both.reshape(2, 2 * outer, 2 * ROWS, kc)
            rc_copy(t).start()

        @pl.when((t >= 1) & (t < CHUNKS + 1))
        def _():
            k = t - 1
            rc_copy(k).wait_recv()
            total = part[k, c].astype(F32) + core_in[k].astype(F32)
            sum_core[k] = total.astype(BF16).reshape(2, outer, 2 * ROWS, kc)
            ry_copy(k).start()

        @pl.when((t >= 2) & (t < CHUNKS + 2))
        def _():
            k = t - 2
            ry_copy(k).wait_recv()
            total = sum_core[k, i].astype(F32) + y_in[k].astype(F32)
            sum_y[k] = total.astype(BF16)
            z_in[k, o] = sum_y[k, o]
            for d in range(1, outer):
                rz_copy(k, z_peer(d), z_peer(d), o, d).start()

        @pl.when(t >= 3)
        def _():
            k = t - 3
            for d in range(1, outer):
                rz_copy(k, z_peer(d), z_peer(d), z_peer(d), d).wait_recv()
            total = jnp.zeros((2 * ROWS, kc), F32)
            for e in range(EXPERTS):
                expert = z_in[k, e * per_expert].astype(F32)
                for m in range(1, per_expert):
                    expert = expert + z_in[k, e * per_expert + m].astype(F32)
                total = total + row_weight[e] * expert
            ffn_ref[:, pl.ds(pl.multiple_of(k * kc, kc), kc)] = total[:ROWS].astype(BF16)
            ffn_ref[:, pl.ds(pl.multiple_of(half + k * kc, kc), kc)] = total[ROWS:].astype(BF16)

        return 0

    lax.fori_loop(0, CHUNKS + 3, sum_step, 0)

    def drain(k, _):
        for d in range(1, outer):
            z_copy(k, o, d).wait_send()
            rz_copy(k, z_peer(d), z_peer(d), o, d).wait_send()
        y_copy(k, i).wait_send()
        c_copy(k, c).wait_send()
        rc_copy(k).wait_send()
        ry_copy(k).wait_send()
        return 0

    lax.fori_loop(0, CHUNKS, drain, 0)


def on_device(
    hidden_states,
    norm_gain,
    expert_ids,
    route_weight,
    w_gate,
    w_up,
    w_down,
    queries,
    key_cache,
    value_cache,
    lengths,
):
    features = hidden_states.shape[1]
    units = w_gate.shape[1]
    outer = lax.axis_size("attn") // 2
    kc = features // 2 // CHUNKS
    blocks = 4 * outer
    vmem = pl.BlockSpec(memory_space=pltpu.VMEM)
    smem = pl.BlockSpec(memory_space=pltpu.SMEM)
    anywhere = pl.BlockSpec(memory_space=pl.ANY)
    dma = pltpu.SemaphoreType.DMA
    return pl.pallas_call(
        functools.partial(kernel, outer),
        out_shape=(
            jax.ShapeDtypeStruct(hidden_states.shape, BF16),
            jax.ShapeDtypeStruct(queries.shape, BF16),
        ),
        in_specs=[vmem] * 4 + [smem] + [anywhere] * 6,
        out_specs=(vmem, vmem),
        scratch_shapes=[
            pltpu.VMEM((CHUNKS, 2 * kc, units), BF16),
            pltpu.VMEM((CHUNKS, 2 * kc, units), BF16),
            pltpu.VMEM((CHUNKS, units, 2 * kc), BF16),
            pltpu.VMEM(queries.shape, BF16),
            pltpu.VMEM(key_cache.shape, BF16),
            pltpu.VMEM(value_cache.shape, BF16),
            pltpu.VMEM((CHUNKS, 2, 2, outer, 2 * ROWS, kc), BF16),
            pltpu.VMEM((blocks * ROWS, units), F32),
            pltpu.VMEM((blocks * ROWS, units), F32),
            pltpu.VMEM((blocks * ROWS, units), BF16),
            pltpu.VMEM((CHUNKS, 2, 2 * outer, 2 * ROWS, kc), BF16),
            pltpu.VMEM((CHUNKS, 2 * outer, 2 * ROWS, kc), BF16),
            pltpu.VMEM((CHUNKS, 2, outer, 2 * ROWS, kc), BF16),
            pltpu.VMEM((CHUNKS, outer, 2 * ROWS, kc), BF16),
            pltpu.VMEM((CHUNKS, outer, 2 * ROWS, kc), BF16),
            pltpu.VMEM((CHUNKS, outer, 2 * ROWS, kc), BF16),
            dma((3,)),
            dma((CHUNKS, 2, 2)),
            dma((CHUNKS, 2)),
            dma((CHUNKS, outer)),
            dma((CHUNKS, outer)),
            dma((CHUNKS,)),
            dma((CHUNKS,)),
            dma((CHUNKS,)),
            dma((CHUNKS,)),
            dma((CHUNKS,)),
            dma((CHUNKS,)),
            dma((CHUNKS,)),
            dma((CHUNKS,)),
            dma((CHUNKS, outer)),
            dma((CHUNKS, outer)),
        ],
        compiler_params=pltpu.CompilerParams(
            collective_id=0, has_side_effects=True, vmem_limit_bytes=60 * 2**20
        ),
    )(
        hidden_states,
        norm_gain.astype(F32).reshape(1, features),
        expert_ids,
        route_weight,
        lengths,
        queries,
        key_cache,
        value_cache,
        w_gate,
        w_up,
        w_down,
    )


def solution(mesh):
    in_specs = (
        P(("parts", "attn", "ffn"), None),
        P(),
        P(("parts", "attn", "ffn"), None),
        P(("parts", "attn", "ffn"), None),
        P(None, ("attn", "ffn")),
        P(None, ("attn", "ffn")),
        P(("attn", "ffn"), None),
        P(("parts", "attn", "ffn"), None),
        P(("parts", "attn", "ffn"), None, None),
        P(("parts", "attn", "ffn"), None, None),
        P(("parts", "attn", "ffn")),
    )
    out_specs = (P(("parts", "attn", "ffn"), None), P(("parts", "attn", "ffn"), None))
    return jax.shard_map(
        on_device, mesh=mesh, in_specs=in_specs, out_specs=out_specs, check_vma=False
    )
```

```python
import functools

import jax
import jax.numpy as jnp
from jax import lax
from jax.experimental import pallas as pl
from jax.experimental.pallas import tpu as pltpu
from jax.sharding import PartitionSpec as P

EXPERTS = 4
HEADS = 64
HEAD_DIM = 256
ROWS = 8
PIECES = 4
CHUNKS = 7
AHEAD = 3
GATHER_Y = 2
GATHER_C = 4
SUM_C = 1
SUM_Y = 4
SUM_Z = 7
F32 = jnp.float32
BF16 = jnp.bfloat16
MESH = pl.DeviceIdType.MESH


def kernel(
    outer,
    hid_ref,
    gain_ref,
    ids_ref,
    rw_ref,
    len_ref,
    q_hbm,
    k_hbm,
    v_hbm,
    wg_hbm,
    wu_hbm,
    wd_hbm,
    ffn_ref,
    attn_ref,
    wg,
    wu,
    wd,
    q_v,
    k_v,
    v_v,
    x,
    gate_acc,
    up_acc,
    hidden,
    part,
    core_in,
    sum_core,
    y_in,
    sum_y,
    z_in,
    att_sem,
    wgu_sem,
    wd_sem,
    z_send,
    z_recv,
    y_send,
    y_recv,
    c_send,
    c_recv,
    rc_send,
    rc_recv,
    ry_send,
    ry_recv,
    rz_send,
    rz_recv,
):
    parts = lax.axis_index("parts")
    attn = lax.axis_index("attn")
    c = lax.axis_index("ffn")
    o = attn // 2
    i = attn % 2
    half = hid_ref.shape[1] // 2
    kc = half // CHUNKS
    blocks = 4 * outer

    def device(o2, i2, c2):
        return (parts, o2 * 2 + i2, c2)

    def z_peer(d):
        return lax.rem(o + d, outer)

    def att_copies():
        return [
            pltpu.make_async_copy(a, b, att_sem.at[n])
            for n, (a, b) in enumerate(((q_hbm, q_v), (k_hbm, k_v), (v_hbm, v_v)))
        ]

    def in_weights(k):
        copies = []
        for h in range(2):
            rows = pl.ds(pl.multiple_of(h * half + k * kc, kc), kc)
            for n, (a, b) in enumerate(((wg_hbm, wg), (wu_hbm, wu))):
                copies.append(
                    pltpu.make_async_copy(
                        a.at[rows, :], b.at[k, pl.ds(h * kc, kc), :], wgu_sem.at[k, n, h]
                    )
                )
        return copies

    def out_weights(k):
        copies = []
        for h in range(2):
            cols = pl.ds(pl.multiple_of(h * half + k * kc, kc), kc)
            copies.append(
                pltpu.make_async_copy(
                    wd_hbm.at[:, cols], wd.at[k, :, pl.ds(h * kc, kc)], wd_sem.at[k, h]
                )
            )
        return copies

    def z_copy(k, o_slot, d):
        return pltpu.make_async_remote_copy(
            src_ref=x.at[k, c, i, o_slot],
            dst_ref=x.at[k, c, i, o_slot],
            send_sem=z_send.at[k, d],
            recv_sem=z_recv.at[k, o_slot],
            device_id=device(z_peer(d), i, c),
            device_id_type=MESH,
        )

    def y_copy(k, i_slot, o_slot):
        return pltpu.make_async_remote_copy(
            src_ref=x.at[k, c, i_slot, o_slot],
            dst_ref=x.at[k, c, i_slot, o_slot],
            send_sem=y_send.at[k, o_slot],
            recv_sem=y_recv.at[k, o_slot],
            device_id=device(o, 1 - i, c),
            device_id_type=MESH,
        )

    def c_copy(k, c_slot):
        return pltpu.make_async_remote_copy(
            src_ref=x.at[k, c_slot],
            dst_ref=x.at[k, c_slot],
            send_sem=c_send.at[k],
            recv_sem=c_recv.at[k],
            device_id=device(o, i, 1 - c),
            device_id_type=MESH,
        )

    def rc_copy(k):
        return pltpu.make_async_remote_copy(
            src_ref=part.at[k, 1 - c],
            dst_ref=core_in.at[k],
            send_sem=rc_send.at[k],
            recv_sem=rc_recv.at[k],
            device_id=device(o, i, 1 - c),
            device_id_type=MESH,
        )

    def ry_copy(k):
        return pltpu.make_async_remote_copy(
            src_ref=sum_core.at[k, 1 - i],
            dst_ref=y_in.at[k],
            send_sem=ry_send.at[k],
            recv_sem=ry_recv.at[k],
            device_id=device(o, 1 - i, c),
            device_id_type=MESH,
        )

    def rz_copy(k, o_src, o_dst, o_slot, d):
        return pltpu.make_async_remote_copy(
            src_ref=sum_y.at[k, o_src],
            dst_ref=z_in.at[k, o_slot],
            send_sem=rz_send.at[k, d],
            recv_sem=rz_recv.at[k, o_slot],
            device_id=device(o_dst, i, c),
            device_id_type=MESH,
        )

    for k in range(2):
        for copy in in_weights(k):
            copy.start()

    barrier = pltpu.get_barrier_semaphore()
    for d in range(1, outer):
        pl.semaphore_signal(
            barrier, inc=1, device_id=device(z_peer(d), i, c), device_id_type=MESH
        )
    pl.semaphore_signal(barrier, inc=1, device_id=device(o, 1 - i, c), device_id_type=MESH)
    pl.semaphore_signal(barrier, inc=1, device_id=device(o, i, 1 - c), device_id_type=MESH)

    for copy in att_copies():
        copy.start()

    as_float = hid_ref[...].astype(F32)
    mean_square = jnp.mean(as_float * as_float, axis=-1, keepdims=True)
    normed = as_float * lax.rsqrt(mean_square + 1e-06) * gain_ref[...].astype(F32).reshape(1, 2 * half)
    for k in range(CHUNKS):
        low = normed[:, k * kc : (k + 1) * kc]
        high = normed[:, half + k * kc : half + (k + 1) * kc]
        x[k, c, i, o] = jnp.concatenate([low, high], axis=0).astype(BF16)

    pl.semaphore_wait(barrier, outer + 1)

    def start_z(k, _):
        for d in range(1, outer):
            z_copy(k, o, d).start()
        y_copy(k, i, o).start()
        return 0

    lax.fori_loop(0, min(AHEAD, CHUNKS), start_z, 0)

    def start_in(k, _):
        for copy in in_weights(k):
            copy.start()
        return 0

    lax.fori_loop(2, CHUNKS, start_in, 0)

    def start_out(k, _):
        for copy in out_weights(k):
            copy.start()
        return 0

    lax.fori_loop(0, CHUNKS, start_out, 0)

    gate_acc[...] = jnp.zeros_like(gate_acc)
    up_acc[...] = jnp.zeros_like(up_acc)
    for copy in att_copies():
        copy.wait()

    heads = HEADS // PIECES
    tall = heads * ROWS
    slots = k_v.shape[1]

    def attention(p):
        def columns(j):
            return pl.ds(pl.multiple_of((p * heads + j) * HEAD_DIM, HEAD_DIM), HEAD_DIM)

        query = jnp.concatenate(
            [q_v[:, columns(j)].astype(F32) for j in range(heads)], axis=0
        ).astype(BF16)
        row = lax.broadcasted_iota(jnp.int32, (tall, slots), 0) & (ROWS - 1)
        filled = jnp.zeros((tall, slots), jnp.int32)
        scores = jnp.zeros((tall, slots), F32)
        for r in range(ROWS):
            own = lax.dot_general(
                query, k_v[r], (((1,), (1,)), ((), ())), preferred_element_type=F32
            )
            scores = jnp.where(row == r, own, scores)
            filled = jnp.where(row == r, len_ref[r], filled)
        scores = scores * HEAD_DIM ** (-0.5)
        visible = lax.broadcasted_iota(jnp.int32, (tall, slots), 1) < filled
        top = jnp.max(jnp.where(visible, scores, -1e30), axis=-1, keepdims=True)
        raised = jnp.where(visible, jnp.exp(scores - top), 0.0)
        probs = raised / jnp.sum(raised, axis=-1, keepdims=True)
        mixed = jnp.zeros((tall, HEAD_DIM), F32)
        for r in range(ROWS):
            own = jnp.where(row == r, probs, 0.0).astype(BF16)
            mixed = mixed + jnp.dot(own, v_v[r], preferred_element_type=F32)
        for j in range(heads):
            attn_ref[:, columns(j)] = mixed[j * ROWS : (j + 1) * ROWS].astype(BF16)

    def gather_step(t, _):
        @pl.when(t < PIECES)
        def _():
            attention(t)

        @pl.when(t < CHUNKS)
        def _():
            for d in range(1, outer):
                z_copy(t, z_peer(d), d).wait_recv()
                y_copy(t, i, z_peer(d)).start()

        @pl.when(t + AHEAD < CHUNKS)
        def _():
            start_z(t + AHEAD, 0)

        @pl.when((t >= GATHER_Y) & (t < CHUNKS + GATHER_Y))
        def _():
            k = t - GATHER_Y
            for d in range(outer):
                y_copy(k, 1 - i, z_peer(d)).wait_recv()
            c_copy(k, c).start()

        @pl.when(t >= GATHER_C)
        def _():
            k = t - GATHER_C
            c_copy(k, 1 - c).wait_recv()
            for copy in in_weights(k):
                copy.wait()
            block = x[k].astype(F32).reshape(blocks, 2 * ROWS, kc)
            low = block[:, :ROWS, :].reshape(blocks * ROWS, kc).astype(BF16)
            high = block[:, ROWS:, :].reshape(blocks * ROWS, kc).astype(BF16)
            rows = jnp.concatenate([low, high], axis=1)
            gate_acc[...] += jnp.dot(rows, wg[k], preferred_element_type=F32)
            up_acc[...] += jnp.dot(rows, wu[k], preferred_element_type=F32)

        return 0

    lax.fori_loop(0, CHUNKS + GATHER_C, gather_step, 0)

    gate = gate_acc[...]
    hidden[...] = (gate / (1.0 + jnp.exp(-gate)) * up_acc[...]).astype(BF16)

    ids = ids_ref[...]
    weights = rw_ref[...]
    place = lax.broadcasted_iota(jnp.int32, (2 * ROWS, ROWS), 0) & (ROWS - 1)
    diagonal = place == lax.broadcasted_iota(jnp.int32, (2 * ROWS, ROWS), 1)
    row_weight = []
    for e in range(EXPERTS):
        along = jnp.sum(jnp.where(ids == e, weights, 0.0), axis=0, keepdims=True)
        row_weight.append(jnp.sum(jnp.where(diagonal, along, 0.0), axis=1, keepdims=True))
    per_expert = outer // EXPERTS

    def sum_step(t, _):
        @pl.when(t < CHUNKS)
        def _():
            for copy in out_weights(t):
                copy.wait()
            down = jnp.dot(hidden[...], wd[t], preferred_element_type=F32)
            low = down[:, :kc].reshape(blocks, ROWS, kc)
            high = down[:, kc:].reshape(blocks, ROWS, kc)
            both = jnp.concatenate([low, high], axis=1).astype(BF16)
            part[t] = both.reshape(2, 2 * outer, 2 * ROWS, kc)
            rc_copy(t).start()

        @pl.when((t >= SUM_C) & (t < CHUNKS + SUM_C))
        def _():
            k = t - SUM_C
            rc_copy(k).wait_recv()
            total = part[k, c].astype(F32) + core_in[k].astype(F32)
            sum_core[k] = total.astype(BF16).reshape(2, outer, 2 * ROWS, kc)
            ry_copy(k).start()

        @pl.when((t >= SUM_Y) & (t < CHUNKS + SUM_Y))
        def _():
            k = t - SUM_Y
            ry_copy(k).wait_recv()
            total = sum_core[k, i].astype(F32) + y_in[k].astype(F32)
            sum_y[k] = total.astype(BF16)
            z_in[k, o] = sum_y[k, o]
            for d in range(1, outer):
                rz_copy(k, z_peer(d), z_peer(d), o, d).start()

        @pl.when(t >= SUM_Z)
        def _():
            k = t - SUM_Z
            for d in range(1, outer):
                rz_copy(k, z_peer(d), z_peer(d), z_peer(d), d).wait_recv()
            total = jnp.zeros((2 * ROWS, kc), F32)
            for e in range(EXPERTS):
                expert = z_in[k, e * per_expert].astype(F32)
                for m in range(1, per_expert):
                    expert = expert + z_in[k, e * per_expert + m].astype(F32)
                total = total + row_weight[e] * expert
            ffn_ref[:, pl.ds(pl.multiple_of(k * kc, kc), kc)] = total[:ROWS].astype(BF16)
            ffn_ref[:, pl.ds(pl.multiple_of(half + k * kc, kc), kc)] = total[ROWS:].astype(BF16)

        return 0

    lax.fori_loop(0, CHUNKS + SUM_Z, sum_step, 0)

    def drain(k, _):
        for d in range(1, outer):
            z_copy(k, o, d).wait_send()
            rz_copy(k, z_peer(d), z_peer(d), o, d).wait_send()
        for d in range(outer):
            y_copy(k, i, z_peer(d)).wait_send()
        c_copy(k, c).wait_send()
        rc_copy(k).wait_send()
        ry_copy(k).wait_send()
        return 0

    lax.fori_loop(0, CHUNKS, drain, 0)


def on_device(
    hidden_states,
    norm_gain,
    expert_ids,
    route_weight,
    w_gate,
    w_up,
    w_down,
    queries,
    key_cache,
    value_cache,
    lengths,
):
    features = hidden_states.shape[1]
    units = w_gate.shape[1]
    outer = lax.axis_size("attn") // 2
    kc = features // 2 // CHUNKS
    blocks = 4 * outer
    vmem = pl.BlockSpec(memory_space=pltpu.VMEM)
    smem = pl.BlockSpec(memory_space=pltpu.SMEM)
    anywhere = pl.BlockSpec(memory_space=pl.ANY)
    dma = pltpu.SemaphoreType.DMA
    return pl.pallas_call(
        functools.partial(kernel, outer),
        out_shape=(
            jax.ShapeDtypeStruct(hidden_states.shape, BF16),
            jax.ShapeDtypeStruct(queries.shape, BF16),
        ),
        in_specs=[vmem] * 4 + [smem] + [anywhere] * 6,
        out_specs=(vmem, vmem),
        scratch_shapes=[
            pltpu.VMEM((CHUNKS, 2 * kc, units), BF16),
            pltpu.VMEM((CHUNKS, 2 * kc, units), BF16),
            pltpu.VMEM((CHUNKS, units, 2 * kc), BF16),
            pltpu.VMEM(queries.shape, BF16),
            pltpu.VMEM(key_cache.shape, BF16),
            pltpu.VMEM(value_cache.shape, BF16),
            pltpu.VMEM((CHUNKS, 2, 2, outer, 2 * ROWS, kc), BF16),
            pltpu.VMEM((blocks * ROWS, units), F32),
            pltpu.VMEM((blocks * ROWS, units), F32),
            pltpu.VMEM((blocks * ROWS, units), BF16),
            pltpu.VMEM((CHUNKS, 2, 2 * outer, 2 * ROWS, kc), BF16),
            pltpu.VMEM((CHUNKS, 2 * outer, 2 * ROWS, kc), BF16),
            pltpu.VMEM((CHUNKS, 2, outer, 2 * ROWS, kc), BF16),
            pltpu.VMEM((CHUNKS, outer, 2 * ROWS, kc), BF16),
            pltpu.VMEM((CHUNKS, outer, 2 * ROWS, kc), BF16),
            pltpu.VMEM((CHUNKS, outer, 2 * ROWS, kc), BF16),
            dma((3,)),
            dma((CHUNKS, 2, 2)),
            dma((CHUNKS, 2)),
            dma((CHUNKS, outer)),
            dma((CHUNKS, outer)),
            dma((CHUNKS, outer)),
            dma((CHUNKS, outer)),
            dma((CHUNKS,)),
            dma((CHUNKS,)),
            dma((CHUNKS,)),
            dma((CHUNKS,)),
            dma((CHUNKS,)),
            dma((CHUNKS,)),
            dma((CHUNKS, outer)),
            dma((CHUNKS, outer)),
        ],
        compiler_params=pltpu.CompilerParams(
            collective_id=0, has_side_effects=True, vmem_limit_bytes=60 * 2**20
        ),
    )(
        hidden_states,
        norm_gain,
        expert_ids.T,
        route_weight.T,
        lengths,
        queries,
        key_cache,
        value_cache,
        w_gate,
        w_up,
        w_down,
    )


def solution(mesh):
    in_specs = (
        P(("parts", "attn", "ffn"), None),
        P(),
        P(("parts", "attn", "ffn"), None),
        P(("parts", "attn", "ffn"), None),
        P(None, ("attn", "ffn")),
        P(None, ("attn", "ffn")),
        P(("attn", "ffn"), None),
        P(("parts", "attn", "ffn"), None),
        P(("parts", "attn", "ffn"), None, None),
        P(("parts", "attn", "ffn"), None, None),
        P(("parts", "attn", "ffn")),
    )
    out_specs = (P(("parts", "attn", "ffn"), None), P(("parts", "attn", "ffn"), None))
    return jax.shard_map(
        on_device, mesh=mesh, in_specs=in_specs, out_specs=out_specs, check_vma=False
    )
```

```python
import functools

import jax
import jax.numpy as jnp
from jax import lax
from jax.experimental import pallas as pl
from jax.experimental.pallas import tpu as pltpu
from jax.sharding import PartitionSpec as P

EXPERTS = 4
HEADS = 64
HEAD_DIM = 256
ROWS = 8
PIECES = 4
CHUNKS = 7
SUM_CHUNKS = 7
AHEAD = 3
GATHER_Y = 3
GATHER_C = 5
SUM_C = 1
SUM_Y = 4
SUM_Z = 7
F32 = jnp.float32
BF16 = jnp.bfloat16
MESH = pl.DeviceIdType.MESH


def kernel(
    outer,
    hid_ref,
    gain_ref,
    ids_ref,
    rw_ref,
    len_ref,
    q_hbm,
    k_hbm,
    v_hbm,
    wg_hbm,
    wu_hbm,
    wd_hbm,
    ffn_ref,
    attn_ref,
    wg,
    wu,
    wd,
    q_v,
    k_v,
    v_v,
    x,
    gate_acc,
    up_acc,
    hidden,
    part,
    core_in,
    sum_core,
    y_in,
    sum_y,
    z_in,
    att_sem,
    wgu_sem,
    wd_sem,
    z_send,
    z_recv,
    y_send,
    y_recv,
    c_send,
    c_recv,
    rc_send,
    rc_recv,
    ry_send,
    ry_recv,
    rz_send,
    rz_recv,
):
    parts = lax.axis_index("parts")
    attn = lax.axis_index("attn")
    c = lax.axis_index("ffn")
    o = attn // 2
    i = attn % 2
    half = hid_ref.shape[1] // 2
    kc = half // CHUNKS
    nc = half // SUM_CHUNKS
    blocks = 4 * outer

    def device(o2, i2, c2):
        return (parts, o2 * 2 + i2, c2)

    def z_peer(d):
        return lax.rem(o + d, outer)

    def att_copies():
        return [
            pltpu.make_async_copy(a, b, att_sem.at[n])
            for n, (a, b) in enumerate(((q_hbm, q_v), (k_hbm, k_v), (v_hbm, v_v)))
        ]

    def in_weights(k):
        copies = []
        for h in range(2):
            rows = pl.ds(pl.multiple_of(h * half + k * kc, kc), kc)
            for n, (a, b) in enumerate(((wg_hbm, wg), (wu_hbm, wu))):
                copies.append(
                    pltpu.make_async_copy(
                        a.at[rows, :], b.at[k, pl.ds(h * kc, kc), :], wgu_sem.at[k, n, h]
                    )
                )
        return copies

    def out_weights(k):
        copies = []
        for h in range(2):
            cols = pl.ds(pl.multiple_of(h * half + k * nc, nc), nc)
            copies.append(
                pltpu.make_async_copy(
                    wd_hbm.at[:, cols], wd.at[k, :, pl.ds(h * nc, nc)], wd_sem.at[k, h]
                )
            )
        return copies

    def z_copy(k, o_slot, d):
        return pltpu.make_async_remote_copy(
            src_ref=x.at[k, c, i, o_slot],
            dst_ref=x.at[k, c, i, o_slot],
            send_sem=z_send.at[k, d],
            recv_sem=z_recv.at[k, o_slot],
            device_id=device(z_peer(d), i, c),
            device_id_type=MESH,
        )

    def y_copy(k, i_slot, o_slot):
        return pltpu.make_async_remote_copy(
            src_ref=x.at[k, c, i_slot, o_slot],
            dst_ref=x.at[k, c, i_slot, o_slot],
            send_sem=y_send.at[k, o_slot],
            recv_sem=y_recv.at[k, o_slot],
            device_id=device(o, 1 - i, c),
            device_id_type=MESH,
        )

    def c_copy(k, c_slot):
        return pltpu.make_async_remote_copy(
            src_ref=x.at[k, c_slot],
            dst_ref=x.at[k, c_slot],
            send_sem=c_send.at[k],
            recv_sem=c_recv.at[k],
            device_id=device(o, i, 1 - c),
            device_id_type=MESH,
        )

    def rc_copy(k):
        return pltpu.make_async_remote_copy(
            src_ref=part.at[k, 1 - c],
            dst_ref=core_in.at[k],
            send_sem=rc_send.at[k],
            recv_sem=rc_recv.at[k],
            device_id=device(o, i, 1 - c),
            device_id_type=MESH,
        )

    def ry_copy(k):
        return pltpu.make_async_remote_copy(
            src_ref=sum_core.at[k, 1 - i],
            dst_ref=y_in.at[k],
            send_sem=ry_send.at[k],
            recv_sem=ry_recv.at[k],
            device_id=device(o, 1 - i, c),
            device_id_type=MESH,
        )

    def rz_copy(k, o_src, o_dst, o_slot, d):
        return pltpu.make_async_remote_copy(
            src_ref=sum_y.at[k, o_src],
            dst_ref=z_in.at[k, o_slot],
            send_sem=rz_send.at[k, d],
            recv_sem=rz_recv.at[k, o_slot],
            device_id=device(o_dst, i, c),
            device_id_type=MESH,
        )

    for k in range(2):
        for copy in in_weights(k):
            copy.start()

    barrier = pltpu.get_barrier_semaphore()
    for d in range(1, outer):
        pl.semaphore_signal(
            barrier, inc=1, device_id=device(z_peer(d), i, c), device_id_type=MESH
        )
    pl.semaphore_signal(barrier, inc=1, device_id=device(o, 1 - i, c), device_id_type=MESH)
    pl.semaphore_signal(barrier, inc=1, device_id=device(o, i, 1 - c), device_id_type=MESH)

    for copy in att_copies():
        copy.start()

    as_float = hid_ref[...].astype(F32)
    mean_square = jnp.mean(as_float * as_float, axis=-1, keepdims=True)
    normed = as_float * lax.rsqrt(mean_square + 1e-06) * gain_ref[...].astype(F32).reshape(1, 2 * half)
    for k in range(CHUNKS):
        low = normed[:, k * kc : (k + 1) * kc]
        high = normed[:, half + k * kc : half + (k + 1) * kc]
        x[k, c, i, o] = jnp.concatenate([low, high], axis=0).astype(BF16)

    pl.semaphore_wait(barrier, outer + 1)

    def start_z(k, _):
        for d in range(1, outer):
            z_copy(k, o, d).start()
        y_copy(k, i, o).start()
        return 0

    lax.fori_loop(0, min(AHEAD, CHUNKS), start_z, 0)

    def start_in(k, _):
        for copy in in_weights(k):
            copy.start()
        return 0

    lax.fori_loop(2, CHUNKS, start_in, 0)

    def start_out(k, _):
        for copy in out_weights(k):
            copy.start()
        return 0

    lax.fori_loop(0, SUM_CHUNKS, start_out, 0)

    gate_acc[...] = jnp.zeros_like(gate_acc)
    up_acc[...] = jnp.zeros_like(up_acc)
    for copy in att_copies():
        copy.wait()

    heads = HEADS // PIECES
    tall = heads * ROWS
    slots = k_v.shape[1]

    def attention(p):
        def columns(j):
            return pl.ds(pl.multiple_of((p * heads + j) * HEAD_DIM, HEAD_DIM), HEAD_DIM)

        query = jnp.concatenate(
            [q_v[:, columns(j)].astype(F32) for j in range(heads)], axis=0
        ).astype(BF16)
        row = lax.broadcasted_iota(jnp.int32, (tall, slots), 0) & (ROWS - 1)
        filled = jnp.zeros((tall, slots), jnp.int32)
        scores = jnp.zeros((tall, slots), F32)
        for r in range(ROWS):
            own = lax.dot_general(
                query, k_v[r], (((1,), (1,)), ((), ())), preferred_element_type=F32
            )
            scores = jnp.where(row == r, own, scores)
            filled = jnp.where(row == r, len_ref[r], filled)
        scores = scores * HEAD_DIM ** (-0.5)
        visible = lax.broadcasted_iota(jnp.int32, (tall, slots), 1) < filled
        top = jnp.max(jnp.where(visible, scores, -1e30), axis=-1, keepdims=True)
        raised = jnp.where(visible, jnp.exp(scores - top), 0.0)
        probs = raised / jnp.sum(raised, axis=-1, keepdims=True)
        mixed = jnp.zeros((tall, HEAD_DIM), F32)
        for r in range(ROWS):
            own = jnp.where(row == r, probs, 0.0).astype(BF16)
            mixed = mixed + jnp.dot(own, v_v[r], preferred_element_type=F32)
        for j in range(heads):
            attn_ref[:, columns(j)] = mixed[j * ROWS : (j + 1) * ROWS].astype(BF16)

    def gather_step(t, _):
        @pl.when(t < PIECES)
        def _():
            attention(t)

        @pl.when(t < CHUNKS)
        def _():
            for d in range(1, outer):
                z_copy(t, z_peer(d), d).wait_recv()
                y_copy(t, i, z_peer(d)).start()

        @pl.when(t + AHEAD < CHUNKS)
        def _():
            start_z(t + AHEAD, 0)

        @pl.when((t >= GATHER_Y) & (t < CHUNKS + GATHER_Y))
        def _():
            k = t - GATHER_Y
            for d in range(outer):
                y_copy(k, 1 - i, z_peer(d)).wait_recv()
            c_copy(k, c).start()

        @pl.when(t >= GATHER_C)
        def _():
            k = t - GATHER_C
            c_copy(k, 1 - c).wait_recv()
            for copy in in_weights(k):
                copy.wait()
            block = x[k].astype(F32).reshape(blocks, 2 * ROWS, kc)
            low = block[:, :ROWS, :].reshape(blocks * ROWS, kc).astype(BF16)
            high = block[:, ROWS:, :].reshape(blocks * ROWS, kc).astype(BF16)
            rows = jnp.concatenate([low, high], axis=1)
            gate_acc[...] += jnp.dot(rows, wg[k], preferred_element_type=F32)
            up_acc[...] += jnp.dot(rows, wu[k], preferred_element_type=F32)

        return 0

    lax.fori_loop(0, CHUNKS + GATHER_C, gather_step, 0)

    gate = gate_acc[...]
    hidden[...] = (gate / (1.0 + jnp.exp(-gate)) * up_acc[...]).astype(BF16)

    ids = ids_ref[...]
    weights = rw_ref[...]
    place = lax.broadcasted_iota(jnp.int32, (2 * ROWS, ROWS), 0) & (ROWS - 1)
    diagonal = place == lax.broadcasted_iota(jnp.int32, (2 * ROWS, ROWS), 1)
    row_weight = []
    for e in range(EXPERTS):
        along = jnp.sum(jnp.where(ids == e, weights, 0.0), axis=0, keepdims=True)
        row_weight.append(jnp.sum(jnp.where(diagonal, along, 0.0), axis=1, keepdims=True))
    per_expert = outer // EXPERTS

    def sum_step(t, _):
        @pl.when(t < SUM_CHUNKS)
        def _():
            for copy in out_weights(t):
                copy.wait()
            down = jnp.dot(hidden[...], wd[t], preferred_element_type=F32)
            low = down[:, :nc].reshape(blocks, ROWS, nc)
            high = down[:, nc:].reshape(blocks, ROWS, nc)
            both = jnp.concatenate([low, high], axis=1).astype(BF16)
            part[t] = both.reshape(2, 2 * outer, 2 * ROWS, nc)
            rc_copy(t).start()

        @pl.when((t >= SUM_C) & (t < SUM_CHUNKS + SUM_C))
        def _():
            k = t - SUM_C
            rc_copy(k).wait_recv()
            total = part[k, c].astype(F32) + core_in[k].astype(F32)
            sum_core[k] = total.astype(BF16).reshape(2, outer, 2 * ROWS, nc)
            ry_copy(k).start()

        @pl.when((t >= SUM_Y) & (t < SUM_CHUNKS + SUM_Y))
        def _():
            k = t - SUM_Y
            ry_copy(k).wait_recv()
            total = sum_core[k, i].astype(F32) + y_in[k].astype(F32)
            sum_y[k] = total.astype(BF16)
            z_in[k, o] = sum_y[k, o]
            for d in range(1, outer):
                rz_copy(k, z_peer(d), z_peer(d), o, d).start()

        @pl.when(t >= SUM_Z)
        def _():
            k = t - SUM_Z
            for d in range(1, outer):
                rz_copy(k, z_peer(d), z_peer(d), z_peer(d), d).wait_recv()
            total = jnp.zeros((2 * ROWS, nc), F32)
            for e in range(EXPERTS):
                expert = z_in[k, e * per_expert].astype(F32)
                for m in range(1, per_expert):
                    expert = expert + z_in[k, e * per_expert + m].astype(F32)
                total = total + row_weight[e] * expert
            ffn_ref[:, pl.ds(pl.multiple_of(k * nc, nc), nc)] = total[:ROWS].astype(BF16)
            ffn_ref[:, pl.ds(pl.multiple_of(half + k * nc, nc), nc)] = total[ROWS:].astype(BF16)

        return 0

    lax.fori_loop(0, SUM_CHUNKS + SUM_Z, sum_step, 0)

    def drain(k, _):
        for d in range(1, outer):
            z_copy(k, o, d).wait_send()
        for d in range(outer):
            y_copy(k, i, z_peer(d)).wait_send()
        c_copy(k, c).wait_send()
        return 0

    lax.fori_loop(0, CHUNKS, drain, 0)

    def drain_sums(k, _):
        for d in range(1, outer):
            rz_copy(k, z_peer(d), z_peer(d), o, d).wait_send()
        rc_copy(k).wait_send()
        ry_copy(k).wait_send()
        return 0

    lax.fori_loop(0, SUM_CHUNKS, drain_sums, 0)


def on_device(
    hidden_states,
    norm_gain,
    expert_ids,
    route_weight,
    w_gate,
    w_up,
    w_down,
    queries,
    key_cache,
    value_cache,
    lengths,
):
    features = hidden_states.shape[1]
    units = w_gate.shape[1]
    outer = lax.axis_size("attn") // 2
    kc = features // 2 // CHUNKS
    nc = features // 2 // SUM_CHUNKS
    blocks = 4 * outer
    vmem = pl.BlockSpec(memory_space=pltpu.VMEM)
    smem = pl.BlockSpec(memory_space=pltpu.SMEM)
    anywhere = pl.BlockSpec(memory_space=pl.ANY)
    dma = pltpu.SemaphoreType.DMA
    return pl.pallas_call(
        functools.partial(kernel, outer),
        out_shape=(
            jax.ShapeDtypeStruct(hidden_states.shape, BF16),
            jax.ShapeDtypeStruct(queries.shape, BF16),
        ),
        in_specs=[vmem] * 4 + [smem] + [anywhere] * 6,
        out_specs=(vmem, vmem),
        scratch_shapes=[
            pltpu.VMEM((CHUNKS, 2 * kc, units), BF16),
            pltpu.VMEM((CHUNKS, 2 * kc, units), BF16),
            pltpu.VMEM((SUM_CHUNKS, units, 2 * nc), BF16),
            pltpu.VMEM(queries.shape, BF16),
            pltpu.VMEM(key_cache.shape, BF16),
            pltpu.VMEM(value_cache.shape, BF16),
            pltpu.VMEM((CHUNKS, 2, 2, outer, 2 * ROWS, kc), BF16),
            pltpu.VMEM((blocks * ROWS, units), F32),
            pltpu.VMEM((blocks * ROWS, units), F32),
            pltpu.VMEM((blocks * ROWS, units), BF16),
            pltpu.VMEM((SUM_CHUNKS, 2, 2 * outer, 2 * ROWS, nc), BF16),
            pltpu.VMEM((SUM_CHUNKS, 2 * outer, 2 * ROWS, nc), BF16),
            pltpu.VMEM((SUM_CHUNKS, 2, outer, 2 * ROWS, nc), BF16),
            pltpu.VMEM((SUM_CHUNKS, outer, 2 * ROWS, nc), BF16),
            pltpu.VMEM((SUM_CHUNKS, outer, 2 * ROWS, nc), BF16),
            pltpu.VMEM((SUM_CHUNKS, outer, 2 * ROWS, nc), BF16),
            dma((3,)),
            dma((CHUNKS, 2, 2)),
            dma((SUM_CHUNKS, 2)),
            dma((CHUNKS, outer)),
            dma((CHUNKS, outer)),
            dma((CHUNKS, outer)),
            dma((CHUNKS, outer)),
            dma((CHUNKS,)),
            dma((CHUNKS,)),
            dma((SUM_CHUNKS,)),
            dma((SUM_CHUNKS,)),
            dma((SUM_CHUNKS,)),
            dma((SUM_CHUNKS,)),
            dma((SUM_CHUNKS, outer)),
            dma((SUM_CHUNKS, outer)),
        ],
        compiler_params=pltpu.CompilerParams(
            collective_id=0, has_side_effects=True, vmem_limit_bytes=60 * 2**20
        ),
    )(
        hidden_states,
        norm_gain,
        expert_ids.T,
        route_weight.T,
        lengths,
        queries,
        key_cache,
        value_cache,
        w_gate,
        w_up,
        w_down,
    )


def solution(mesh):
    in_specs = (
        P(("parts", "attn", "ffn"), None),
        P(),
        P(("parts", "attn", "ffn"), None),
        P(("parts", "attn", "ffn"), None),
        P(None, ("attn", "ffn")),
        P(None, ("attn", "ffn")),
        P(("attn", "ffn"), None),
        P(("parts", "attn", "ffn"), None),
        P(("parts", "attn", "ffn"), None, None),
        P(("parts", "attn", "ffn"), None, None),
        P(("parts", "attn", "ffn")),
    )
    out_specs = (P(("parts", "attn", "ffn"), None), P(("parts", "attn", "ffn"), None))
    return jax.shard_map(
        on_device, mesh=mesh, in_specs=in_specs, out_specs=out_specs, check_vma=False
    )
```
